128 devices in a mesh: dp: 4 (over z), cuts: 32 (over x, y, core).
Axes of the slice: x: 4, y: 4, z: 4, core: 2. Of those that a mesh axis runs over, the one named last changes fastest.
Arguments:
- tokens: bfloat16 [3072, 6144], P('dp', 'cuts'), may hold values from -6 to 6
- cotangent: bfloat16 [3072, 6144], P('dp', 'cuts'), may hold values from -6 to 6
- expert_ids: int32 [3072, 2], P('dp'), may hold values from 0 to 7, as said below
- gates: float32 [3072, 2], P('dp'), may hold values from 0.1 to 0.9
- w_gate: bfloat16 [6144, 16384], P('dp', 'cuts'), may hold values from -0.078125 to 0.078125
- w_up: bfloat16 [6144, 16384], P('dp', 'cuts'), may hold values from -0.078125 to 0.078125
- w_down: bfloat16 [6144, 16384], P('dp', 'cuts'), may hold values from -0.046875 to 0.046875
Outputs:
- grad_tokens: bfloat16 [3072, 6144], P('dp', 'cuts')
- grad_gate: bfloat16 [6144, 16384], P('dp', 'cuts')
- grad_up: bfloat16 [6144, 16384], P('dp', 'cuts')
- grad_down: bfloat16 [6144, 16384], P('dp', 'cuts')
The draws below stay inside these ranges and needn't reach their ends.
Inputs may be any that keep to these rules, and one draw needn't show every extreme that they name: `expert_ids`: each token names two different experts. In each token group at most 384 tokens name expert 0, and in some group exactly 384 do.
All inputs are finite; a program needn't handle non-finite values.
Results may differ from the reference program's by a relative error of at most 0.023.
Values may be sent and summed in bfloat16 or wider, within the bound.
No kernel may reach another device: no remote copies, remote signals or barrier semaphores. Data moves between devices by JAX's collectives and lax.ppermute only.
A program may use at most 128 MiB of HBM per device.

```python
import jax
import jax.numpy as jnp
from jax import lax

D = 6144
FF = 16384
N_EXPERTS = 8
TOK_GRP = 768
CAP = 384
TOKENS = 3072
N_DP = 4


def draw_expert_ids(key, part):
    key = jax.random.fold_in(key, 7)
    subkeys = jax.random.split(key, 6)
    group_count = TOKENS // TOK_GRP
    group_loads = jax.random.randint(subkeys[0], (group_count,), CAP // 4, CAP + 1)
    fullest = jax.random.randint(subkeys[1], (), 0, group_count)
    group_loads = jnp.where(jnp.arange(group_count) == fullest, CAP, group_loads)
    orderings = jax.vmap(lambda subkey: jax.random.permutation(subkey, TOK_GRP))(jax.random.split(subkeys[2], group_count))
    chosen = (orderings < group_loads[:, None]).reshape(TOKENS)
    other_id = jax.random.randint(subkeys[3], (TOKENS,), 1, N_EXPERTS)
    second_id = 1 + (other_id - 1 + jax.random.randint(subkeys[4], (TOKENS,), 1, N_EXPERTS - 1)) % (N_EXPERTS - 1)
    first_id = jnp.where(chosen, 0, other_id)
    swapped = jax.random.randint(subkeys[5], (TOKENS,), 0, 2) == 1
    left_ids = jnp.where(swapped, second_id, first_id)
    right_ids = jnp.where(swapped, first_id, second_id)
    return jnp.stack([left_ids, right_ids], axis=1).astype(jnp.int32)


def shard_levels(stream_key, extent, cuts, low, largest):
    gain = 1.0
    for position, shards_of in cuts:
        steps = jax.random.uniform(jax.random.fold_in(jax.random.fold_in(stream_key, 6), position), (shards_of,), jnp.float32, low / len(cuts), largest / len(cuts))
        gain = gain * jnp.repeat(jnp.exp(steps), extent[position] // shards_of).reshape((-1,) + (1,) * (len(extent) - 1 - position))
    return gain


def bell_draw(rng, shape, deviation, reach, shards=(), kind=jnp.bfloat16):
    result = deviation * jax.random.normal(rng, shape, jnp.float32)
    if shards:
        result = result * shard_levels(rng, shape, shards, -0.22, 0.18)
    return jnp.clip(result, -reach, reach).astype(kind)


def setup_inputs(seed: int = 0) -> dict:
    key_list = jax.random.split(jax.random.key(seed), 8)
    return {
        "tokens": bell_draw(key_list[0], (TOKENS, D), 1.0, 6.0, ((0, 4), (1, 32))),
        "cotangent": bell_draw(key_list[1], (TOKENS, D), 1.0, 6.0, ((0, 4), (1, 32))),
        "expert_ids": draw_expert_ids(jax.random.fold_in(key_list[7], 71), 0),
        "gates": jnp.clip(0.1 + 0.79999997 * jax.random.uniform(key_list[3], (TOKENS, 2), jnp.float32) ** shard_levels(key_list[3], (TOKENS, 2), ((0, 4),), -0.2, 0.2), 0.1, 0.9),
        "w_gate": bell_draw(key_list[4], (D, FF), D ** -0.5, 0.078125, ((0, 4), (1, 32))),
        "w_up": bell_draw(key_list[5], (D, FF), D ** -0.5, 0.078125, ((0, 4), (1, 32))),
        "w_down": bell_draw(key_list[6], (D, FF), FF ** -0.5, 0.046875, ((0, 4), (1, 32))),
    }


def swiglu_backward(gate_pre, up_pre, grad_hidden):
    logistic = jax.nn.sigmoid(gate_pre)
    activated = gate_pre * logistic
    hidden = (activated * up_pre).astype(jnp.bfloat16)
    grad_up = (grad_hidden * activated).astype(jnp.bfloat16)
    grad_gate = (grad_hidden * up_pre * logistic * (1.0 + gate_pre * (1.0 - logistic))).astype(jnp.bfloat16)
    return grad_gate, grad_up, hidden


def group_summed(left_side, right_side):
    summed = jnp.zeros((left_side.shape[2], right_side.shape[2]), jnp.float32)
    for group in range(N_DP):
        group_term = lax.dot_general(left_side[group], right_side[group], (((0,), (0,)), ((), ())), preferred_element_type=jnp.float32)
        rounded = lax.optimization_barrier(group_term.astype(jnp.bfloat16))
        summed = summed + rounded.astype(jnp.float32)
    return summed.astype(jnp.bfloat16)


def reference(tokens, cotangent, expert_ids, gates, w_gate, w_up, w_down):
    routed = expert_ids == 0
    routed_weight = jnp.sum(jnp.where(routed, gates, jnp.float32(0.0)), axis=1)
    is_routed = jnp.any(routed, axis=1).reshape(N_DP, TOK_GRP)
    slot_rank = jnp.cumsum(is_routed.astype(jnp.int32), axis=1) - 1
    slot_index = jnp.arange(CAP, dtype=jnp.int32)
    selector = ((slot_rank[:, None, :] == slot_index[None, :, None]) & is_routed[:, None, :]).astype(jnp.float32)
    high = lax.Precision.HIGHEST
    token_blocks = tokens.reshape(N_DP, TOK_GRP, D).astype(jnp.float32)
    cot_blocks = cotangent.reshape(N_DP, TOK_GRP, D).astype(jnp.float32)
    slot_x = jnp.einsum("gct,gtd->gcd", selector, token_blocks, precision=high).astype(jnp.bfloat16)
    slot_dy = jnp.einsum("gct,gtd->gcd", selector, cot_blocks, precision=high).astype(jnp.bfloat16)
    slot_weight = jnp.einsum("gct,gt->gc", selector, routed_weight.reshape(N_DP, TOK_GRP), precision=high)
    scaled = (slot_weight[:, :, None] * slot_dy.astype(jnp.float32)).astype(jnp.bfloat16)
    flat_x = slot_x.reshape(N_DP * CAP, D)
    flat_scaled = scaled.reshape(N_DP * CAP, D)
    gate_pre = jnp.dot(flat_x, w_gate, preferred_element_type=jnp.float32)
    up_pre = jnp.dot(flat_x, w_up, preferred_element_type=jnp.float32)
    grad_hidden = jnp.dot(flat_scaled, w_down, preferred_element_type=jnp.float32)
    dgate, dup, hidden = swiglu_backward(gate_pre, up_pre, grad_hidden)
    contract_units = (((1,), (1,)), ((), ()))
    slot_grad = lax.dot_general(dgate, w_gate, contract_units, preferred_element_type=jnp.float32)
    slot_grad = slot_grad + lax.dot_general(dup, w_up, contract_units, preferred_element_type=jnp.float32)
    placed = jnp.einsum("gct,gcd->gtd", selector, slot_grad.reshape(N_DP, CAP, D), precision=high)
    grad_tokens = placed.reshape(TOKENS, D).astype(jnp.bfloat16)
    dgate_groups = dgate.reshape(N_DP, CAP, FF)
    dup_groups = dup.reshape(N_DP, CAP, FF)
    hidden_groups = hidden.reshape(N_DP, CAP, FF)
    grad_gate = group_summed(slot_x, dgate_groups)
    grad_up = group_summed(slot_x, dup_groups)
    grad_down = group_summed(scaled, hidden_groups)
    return grad_tokens, grad_gate, grad_up, grad_down
```

```python
import functools

import jax
import jax.numpy as jnp
from jax import lax
from jax.experimental import pallas as pl
from jax.experimental.pallas import tpu as pltpu
from jax.sharding import Mesh
from jax.sharding import PartitionSpec as P

CAP = 384
BF = jnp.bfloat16
F32 = jnp.float32
N = 4


def index_of(z, x, y, c):
    return ((z * N + x) * N + y) * 2 + c


def every(function):
    pairs = []
    for z in range(N):
        for x in range(N):
            for y in range(N):
                for c in range(2):
                    pairs.append((index_of(z, x, y, c), index_of(*function(z, x, y, c))))
    return pairs


def move(a, function):
    return lax.ppermute(a, ("z", "x", "y", "core"), every(function))


def shift(order, j):
    def function(z, x, y, c):
        return (z, x, (y + j) % N, c) if order[c] == "y" else (z, (x + j) % N, y, c)

    return function


def other_core(a):
    return lax.ppermute(a, "core", [(0, 1), (1, 0)])


def along_z(a, k):
    return lax.ppermute(a, "z", [(i, (i + k) % N) for i in range(N)])


def block(a, index):
    return lax.dynamic_index_in_dim(a, index % N, 0, keepdims=False)


def put(a, value, index):
    return lax.dynamic_update_slice(a, value[None], (index % N,) + (0,) * value.ndim)


def cost(flops, nbytes):
    return pl.CostEstimate(flops=int(flops), bytes_accessed=int(nbytes), transcendentals=0)


def params(mib):
    return pltpu.CompilerParams(vmem_limit_bytes=mib * 1024 * 1024)


def dot(a, b, dims):
    return lax.dot_general(a, b, (dims, ((), ())), preferred_element_type=F32)


def places(where):
    core, x, y = where[0], where[1], where[2]
    for first, side in ((0, core), (N, 1 - core)):
        for j in range(N):
            m = lax.rem(jnp.where(side == 0, y, x) + (N - j), N)
            for b in range(N):
                n = lax.rem(jnp.where(side == 0, x, y) + (N - b), N)
                group = jnp.where(side == 0, n, m)
                row = jnp.where(side == 0, 2 * m, 2 * n + 1)
                yield first + j, b, group, pl.multiple_of(row * 192, 192)


def forward_kernel(count, where, *refs):
    pieces = refs[: 2 * N]
    weights = refs[2 * N : 2 * N + count]
    out, xg_out, xg, held, out_sems, x_sems = refs[2 * N + count :]
    for j, b, group, row in places(where):
        xg[group, pl.ds(row, 192), :] = pieces[j][b]
    stores = []
    for g in range(N):
        copy = pltpu.make_async_copy(xg.at[g], xg_out.at[g], x_sems.at[g])
        copy.start()
        stores.append(copy)
    for p in range(2):
        a = jnp.concatenate([xg[2 * p], xg[2 * p + 1]], axis=1)
        for k in range(count):
            total = dot(weights[k][...], a, ((0,), (0,))).astype(BF)
            for h in range(2):
                g = 2 * p + h
                held[g, k] = total[:, h * CAP : (h + 1) * CAP]
                copy = pltpu.make_async_copy(
                    held.at[g, k], out.at[g, k], out_sems.at[g * count + k]
                )
                copy.start()
                stores.append(copy)
    for copy in stores:
        copy.wait()


def forward(where, pieces, *weights):
    count = len(weights)
    vm = pl.BlockSpec(memory_space=pltpu.VMEM)
    return pl.pallas_call(
        functools.partial(forward_kernel, count),
        out_shape=(
            jax.ShapeDtypeStruct((N, count, 512, CAP), BF),
            jax.ShapeDtypeStruct((N, 1536, CAP), BF),
        ),
        in_specs=[pl.BlockSpec(memory_space=pltpu.SMEM)] + [vm] * (2 * N + count),
        out_specs=(pl.BlockSpec(memory_space=pl.ANY), pl.BlockSpec(memory_space=pl.ANY)),
        scratch_shapes=[
            pltpu.VMEM((N, 1536, CAP), BF),
            pltpu.VMEM((N, count, 512, CAP), BF),
            pltpu.SemaphoreType.DMA((N * count,)),
            pltpu.SemaphoreType.DMA((N,)),
        ],
        compiler_params=params(28),
        cost_estimate=cost(count * 2 * 1536 * 1536 * 512, 5e6 * (1 + count)),
        name="forward_%d" % count,
    )(where, *pieces, *weights)


def slot_kernel(where, wg, wu, dgu, out):
    side = where[0]
    w = jnp.concatenate(
        [
            jnp.concatenate(
                [r[pl.ds(pl.multiple_of((2 * f + side) * 192, 192), 192), :] for f in range(N)]
            )
            for r in (wg, wu)
        ],
        axis=1,
    )
    for p in range(2):
        d = jnp.concatenate(
            [jnp.concatenate([dgu[2 * p + h, k] for k in range(2)]) for h in range(2)], axis=1
        )
        total = dot(w, d, ((1,), (0,))).astype(BF)
        for h in range(2):
            g = 2 * p + h
            for f in range(N):
                index = jnp.where(side == 0, f * N + g, g * N + f)
                out[index] = total[f * 192 : (f + 1) * 192, h * CAP : (h + 1) * CAP]


def slot_partials(side, wg, wu, dgu):
    vm = pl.BlockSpec(memory_space=pltpu.VMEM)
    return pl.pallas_call(
        slot_kernel,
        out_shape=jax.ShapeDtypeStruct((N * N, 192, CAP), BF),
        in_specs=[pl.BlockSpec(memory_space=pltpu.SMEM)] + [vm] * 3,
        out_specs=vm,
        compiler_params=params(24),
        cost_estimate=cost(2 * 1536 * 1536 * 512, 9e6),
        name="slot_partials",
    )(side.reshape(1).astype(jnp.int32), wg, wu, dgu)


def weight_kernel(x, d, *outs):
    for k, out in enumerate(outs):
        total = 0.0
        for p in range(2):
            left = jnp.concatenate([x[2 * p], x[2 * p + 1]], axis=1)
            right = jnp.concatenate([d[2 * p, k], d[2 * p + 1, k]], axis=1)
            total += dot(left, right, ((1,), (1,)))
        out[...] = total.astype(BF)


def weight_grads(x, d):
    n = d.shape[1]
    rows = 256
    return pl.pallas_call(
        weight_kernel,
        grid=(1536 // rows,),
        out_shape=[jax.ShapeDtypeStruct((1536, 512), BF)] * n,
        in_specs=[
            pl.BlockSpec((N, rows, CAP), lambda i: (0, i, 0)),
            pl.BlockSpec((N, n, 512, CAP), lambda i: (0, 0, 0, 0)),
        ],
        out_specs=[pl.BlockSpec((rows, 512), lambda i: (i, 0))] * n,
        compiler_params=params(20),
        cost_estimate=cost(n * 2 * 1536 * 1536 * 512, 8e6),
        name="weight_grads_%d" % n,
    )(x, d)


def sum_over_z(a, z):
    far = block(a, z + 2)
    up_half = along_z(far[0], 1)
    down_half = along_z(far[1], 3)
    right, left = block(a, z + 1), block(a, z + 3)
    right = jnp.stack([right[0] + up_half, right[1]])
    left = jnp.stack([left[0], left[1] + down_half])
    from_left, from_right = along_z(right, 1), along_z(left, 3)
    return block(a, z).astype(F32) + from_left.astype(F32) + from_right.astype(F32)


def neighbours_over_z(a):
    return along_z(a, 1), along_z(a, 3)


def gather_over_z(a, near, z):
    from_left, from_right = near
    far0 = along_z(from_left[0], 1)
    far1 = along_z(from_right[1], 3)
    out = jnp.zeros((N,) + a.shape, a.dtype)
    out = put(out, a, z)
    out = put(out, from_left, z + 3)
    out = put(out, from_right, z + 1)
    return put(out, jnp.stack([far0, far1]), z + 2)


def sum_of(arrays):
    return sum(a.astype(F32) for a in arrays)


def per_device(tokens, cotangent, expert_ids, gates, w_gate, w_up, w_down):
    z, x, y, core = (lax.axis_index(a) for a in ("z", "x", "y", "core"))
    where = jnp.stack([core, (x - z + N) % N, y]).astype(jnp.int32)
    routed = expert_ids == 0
    routed_weight = jnp.sum(jnp.where(routed, gates, 0.0), axis=1)
    is_routed = jnp.any(routed, axis=1)
    slot_rank = jnp.cumsum(is_routed.astype(jnp.int32)) - 1
    slot_index = jnp.arange(CAP, dtype=jnp.int32)
    selector = (slot_rank[None, :] == slot_index[:, None]) & is_routed[None, :]
    picker = selector.astype(BF)
    slot_weight = jnp.sum(jnp.where(selector, routed_weight[None, :], 0.0), axis=1)
    x_slots = dot(tokens, picker, ((0,), (1,))).astype(BF)
    dy_slots = dot(cotangent, picker, ((0,), (1,))).astype(BF)
    scaled = (slot_weight[None, :] * dy_slots.astype(F32)).astype(BF)

    both = jnp.stack([x_slots, scaled])
    both = move(both, lambda z, x, y, c: (x, (z + x) % N, y, c))
    hop = [both] + [move(both, shift("xy", j)) for j in range(1, N)]
    x_held = jnp.stack([a[0] for a in hop])
    dy_held = jnp.stack([a[1] for a in hop])
    x_own = [x_held] + [move(x_held, shift("yx", j)) for j in range(1, N)]
    x_pieces = x_own + [other_core(a) for a in x_own]
    dy_held, _ = lax.optimization_barrier((dy_held, x_own[2]))
    dy_own = [dy_held] + [move(dy_held, shift("yx", j)) for j in range(1, N)]
    dy_pieces = dy_own + [other_core(a) for a in dy_own]

    gu, xg = forward(where, x_pieces, w_gate, w_up)
    gh, dyg = forward(where, dy_pieces, w_down)
    gate_up = sum_over_z(gu, z)
    gate_pre, up_pre = gate_up[0], gate_up[1]
    grad_hidden = sum_over_z(gh.reshape(N, 2, 256, CAP), z).reshape(512, CAP)

    logistic = jax.nn.sigmoid(gate_pre)
    activated = gate_pre * logistic
    hidden = (activated * up_pre).astype(BF)
    dup = (grad_hidden * activated).astype(BF)
    dgate = (grad_hidden * up_pre * logistic * (1.0 + gate_pre * (1.0 - logistic))).astype(BF)

    dgu = jnp.stack([dgate, dup])
    near = neighbours_over_z(dgu)
    dgu = gather_over_z(dgu, near, z)
    hidden, _ = lax.optimization_barrier((hidden.reshape(2, 256, CAP), near[0]))
    hidden_near = neighbours_over_z(hidden)

    theirs = other_core(slot_partials(1 - core, w_gate, w_up, dgu))
    total = slot_partials(core, w_gate, w_up, dgu)
    total = sum_of((total, theirs)).astype(BF).reshape(N, N, 192, CAP)
    dgu, total = lax.optimization_barrier((dgu, total))
    total = plane_sum(total, jnp.where(core == 0, y, x), "yx")
    hidden_near, _ = lax.optimization_barrier((hidden_near, total))
    hidden_all = gather_over_z(hidden, hidden_near, z).reshape(N, 1, 512, CAP)
    grad_gate, grad_up = weight_grads(xg, dgu)
    total, grad_gate = lax.optimization_barrier((total, grad_gate))
    total = plane_sum(total, jnp.where(core == 0, x, y), "xy")
    (grad_down,) = weight_grads(dyg, hidden_all)
    slot_grad = move(total, lambda z, x, y, c: (x, z, y, c))
    grad_tokens = dot(picker, slot_grad, ((0,), (1,))).astype(BF)
    return grad_tokens, grad_gate, grad_up, grad_down


def plane_sum(a, index, order):
    got = [block(a, index)]
    got += [move(block(a, index + j), shift(order, j)) for j in range(1, N)]
    return sum_of(got).astype(BF)


def solution(mesh):
    fine = Mesh(mesh.devices.reshape(N, N, N, 2), ("z", "x", "y", "core"))
    cuts = ("x", "y", "core")
    split, rows = P("z", cuts), P("z", None)
    return jax.shard_map(
        per_device,
        mesh=fine,
        in_specs=(split, split, rows, rows, split, split, split),
        out_specs=(split, split, split, split),
        check_vma=False,
    )
```

```python
import functools

import jax
import jax.numpy as jnp
from jax import lax
from jax.experimental import pallas as pl
from jax.experimental.pallas import tpu as pltpu
from jax.sharding import Mesh
from jax.sharding import PartitionSpec as P

CAP = 384
BF = jnp.bfloat16
F32 = jnp.float32
N = 4


def index_of(z, x, y, c):
    return ((z * N + x) * N + y) * 2 + c


def every(function):
    pairs = []
    for z in range(N):
        for x in range(N):
            for y in range(N):
                for c in range(2):
                    pairs.append((index_of(z, x, y, c), index_of(*function(z, x, y, c))))
    return pairs


def move(a, function):
    return lax.ppermute(a, ("z", "x", "y", "core"), every(function))


def shift(order, j):
    def function(z, x, y, c):
        return (z, x, (y + j) % N, c) if order[c] == "y" else (z, (x + j) % N, y, c)

    return function


def other_core(a):
    return lax.ppermute(a, "core", [(0, 1), (1, 0)])


def along_z(a, k):
    return lax.ppermute(a, "z", [(i, (i + k) % N) for i in range(N)])


def block(a, index):
    return lax.dynamic_index_in_dim(a, index % N, 0, keepdims=False)


def put(a, value, index):
    return lax.dynamic_update_slice(a, value[None], (index % N,) + (0,) * value.ndim)


def cost(flops, nbytes):
    return pl.CostEstimate(flops=int(flops), bytes_accessed=int(nbytes), transcendentals=0)


def params(mib):
    return pltpu.CompilerParams(vmem_limit_bytes=mib * 1024 * 1024)


def dot(a, b, dims):
    return lax.dot_general(a, b, (dims, ((), ())), preferred_element_type=F32)


def places(where):
    core, x, y = where[0], where[1], where[2]
    for operand, side in ((0, core), (1, 1 - core)):
        for j in range(N):
            m = lax.rem(jnp.where(side == 0, y, x) + (N - j), N)
            for b in range(N):
                n = lax.rem(jnp.where(side == 0, x, y) + (N - b), N)
                group = jnp.where(side == 0, n, m)
                row = jnp.where(side == 0, 2 * m, 2 * n + 1)
                yield operand, j, b, group, pl.multiple_of(row * 192, 192)


def forward_kernel(count, where, *refs):
    pieces, weights = refs[:2], refs[2 : 2 + count]
    out, xg = refs[2 + count :]
    for operand, j, b, group, row in places(where):
        xg[group, pl.ds(row, 192), :] = pieces[operand][j, b]
    for p in range(2):
        a = jnp.concatenate([xg[2 * p], xg[2 * p + 1]], axis=1)
        for k in range(count):
            total = dot(weights[k][...], a, ((0,), (0,))).astype(BF)
            for h in range(2):
                out[2 * p + h, k] = total[:, h * CAP : (h + 1) * CAP]


def forward(where, own, sib, *weights):
    count = len(weights)
    vm = pl.BlockSpec(memory_space=pltpu.VMEM)
    return pl.pallas_call(
        functools.partial(forward_kernel, count),
        out_shape=(
            jax.ShapeDtypeStruct((N, count, 512, CAP), BF),
            jax.ShapeDtypeStruct((N, 1536, CAP), BF),
        ),
        in_specs=[pl.BlockSpec(memory_space=pltpu.SMEM)] + [vm] * (2 + count),
        out_specs=(vm, vm),
        compiler_params=params(24),
        cost_estimate=cost(count * 2 * 1536 * 1536 * 512, 5e6 * (1 + count)),
        name="forward_%d" % count,
    )(where, own, sib, *weights)


def slot_kernel(where, wg, wu, dgu, out):
    side = where[0]
    w = jnp.concatenate(
        [
            jnp.concatenate(
                [r[pl.ds(pl.multiple_of((2 * f + side) * 192, 192), 192), :] for f in range(N)]
            )
            for r in (wg, wu)
        ],
        axis=1,
    )
    for p in range(2):
        d = jnp.concatenate(
            [jnp.concatenate([dgu[2 * p + h, k] for k in range(2)]) for h in range(2)], axis=1
        )
        total = dot(w, d, ((1,), (0,))).astype(BF)
        for h in range(2):
            g = 2 * p + h
            for f in range(N):
                index = jnp.where(side == 0, f * N + g, g * N + f)
                out[index] = total[f * 192 : (f + 1) * 192, h * CAP : (h + 1) * CAP]


def slot_partials(side, wg, wu, dgu):
    vm = pl.BlockSpec(memory_space=pltpu.VMEM)
    return pl.pallas_call(
        slot_kernel,
        out_shape=jax.ShapeDtypeStruct((N * N, 192, CAP), BF),
        in_specs=[pl.BlockSpec(memory_space=pltpu.SMEM)] + [vm] * 3,
        out_specs=vm,
        compiler_params=params(24),
        cost_estimate=cost(2 * 1536 * 1536 * 512, 9e6),
        name="slot_partials",
    )(side.reshape(1).astype(jnp.int32), wg, wu, dgu)


def weight_kernel(x, d, *outs):
    for k, out in enumerate(outs):
        total = 0.0
        for p in range(2):
            left = jnp.concatenate([x[2 * p], x[2 * p + 1]], axis=1)
            right = jnp.concatenate([d[2 * p, k], d[2 * p + 1, k]], axis=1)
            total += dot(left, right, ((1,), (1,)))
        out[...] = total.astype(BF)


def weight_grads(x, d):
    n = d.shape[1]
    rows = 256
    return pl.pallas_call(
        weight_kernel,
        grid=(1536 // rows,),
        out_shape=[jax.ShapeDtypeStruct((1536, 512), BF)] * n,
        in_specs=[
            pl.BlockSpec((N, rows, CAP), lambda i: (0, i, 0)),
            pl.BlockSpec((N, n, 512, CAP), lambda i: (0, 0, 0, 0)),
        ],
        out_specs=[pl.BlockSpec((rows, 512), lambda i: (i, 0))] * n,
        compiler_params=params(20),
        cost_estimate=cost(n * 2 * 1536 * 1536 * 512, 8e6),
        name="weight_grads_%d" % n,
    )(x, d)


def sum_over_z(a, z):
    far = block(a, z + 2)
    up_half = along_z(far[0], 1)
    down_half = along_z(far[1], 3)
    right, left = block(a, z + 1), block(a, z + 3)
    right = jnp.stack([right[0] + up_half, right[1]])
    left = jnp.stack([left[0], left[1] + down_half])
    from_left, from_right = along_z(right, 1), along_z(left, 3)
    return block(a, z).astype(F32) + from_left.astype(F32) + from_right.astype(F32)


def neighbours_over_z(a):
    return along_z(a, 1), along_z(a, 3)


def gather_over_z(a, near, z):
    from_left, from_right = near
    far0 = along_z(from_left[0], 1)
    far1 = along_z(from_right[1], 3)
    out = jnp.zeros((N,) + a.shape, a.dtype)
    out = put(out, a, z)
    out = put(out, from_left, z + 3)
    out = put(out, from_right, z + 1)
    return put(out, jnp.stack([far0, far1]), z + 2)


def sum_of(arrays):
    return sum(a.astype(F32) for a in arrays)


def per_device(tokens, cotangent, expert_ids, gates, w_gate, w_up, w_down):
    z, x, y, core = (lax.axis_index(a) for a in ("z", "x", "y", "core"))
    where = jnp.stack([core, (x - z + N) % N, y]).astype(jnp.int32)
    routed = expert_ids == 0
    routed_weight = jnp.sum(jnp.where(routed, gates, 0.0), axis=1)
    is_routed = jnp.any(routed, axis=1)
    slot_rank = jnp.cumsum(is_routed.astype(jnp.int32)) - 1
    slot_index = jnp.arange(CAP, dtype=jnp.int32)
    selector = (slot_rank[None, :] == slot_index[:, None]) & is_routed[None, :]
    picker = selector.astype(BF)
    slot_weight = jnp.sum(jnp.where(selector, routed_weight[None, :], 0.0), axis=1)
    x_slots = dot(tokens, picker, ((0,), (1,))).astype(BF)
    dy_slots = dot(cotangent, picker, ((0,), (1,))).astype(BF)
    scaled = (slot_weight[None, :] * dy_slots.astype(F32)).astype(BF)

    both = jnp.stack([x_slots, scaled])
    both = move(both, lambda z, x, y, c: (x, (z + x) % N, y, c))
    hop = [both] + [move(both, shift("xy", j)) for j in range(1, N)]
    x_held = jnp.stack([a[0] for a in hop])
    dy_held = jnp.stack([a[1] for a in hop])
    x_own = [x_held] + [move(x_held, shift("yx", j)) for j in range(1, N)]
    dy_held, _ = lax.optimization_barrier((dy_held, x_own[2]))
    x_own = jnp.stack(x_own)
    x_sib = other_core(x_own)
    gu, xg = forward(where, x_own, x_sib, w_gate, w_up)
    dy_own = [dy_held] + [move(dy_held, shift("yx", j)) for j in range(1, N)]
    dy_own, gu = lax.optimization_barrier((dy_own, gu))
    dy_own = jnp.stack(dy_own)
    dy_sib = other_core(dy_own)
    gh, dyg = forward(where, dy_own, dy_sib, w_down)
    gate_up = sum_over_z(gu, z)
    gate_pre, up_pre = gate_up[0], gate_up[1]
    grad_hidden = sum_over_z(gh.reshape(N, 2, 256, CAP), z).reshape(512, CAP)

    logistic = jax.nn.sigmoid(gate_pre)
    activated = gate_pre * logistic
    hidden = (activated * up_pre).astype(BF)
    dup = (grad_hidden * activated).astype(BF)
    dgate = (grad_hidden * up_pre * logistic * (1.0 + gate_pre * (1.0 - logistic))).astype(BF)

    dgu = jnp.stack([dgate, dup])
    near = neighbours_over_z(dgu)
    dgu = gather_over_z(dgu, near, z)
    hidden, _ = lax.optimization_barrier((hidden.reshape(2, 256, CAP), near[0]))
    hidden_near = neighbours_over_z(hidden)

    theirs = other_core(slot_partials(1 - core, w_gate, w_up, dgu))
    total = slot_partials(core, w_gate, w_up, dgu)
    total = sum_of((total, theirs)).astype(BF).reshape(N, N, 192, CAP)
    dgu, total = lax.optimization_barrier((dgu, total))
    total = plane_sum(total, jnp.where(core == 0, y, x), "yx")
    hidden_near, _ = lax.optimization_barrier((hidden_near, total))
    hidden_all = gather_over_z(hidden, hidden_near, z).reshape(N, 1, 512, CAP)
    grad_gate, grad_up = weight_grads(xg, dgu)
    total, grad_gate = lax.optimization_barrier((total, grad_gate))
    total = plane_sum(total, jnp.where(core == 0, x, y), "xy")
    (grad_down,) = weight_grads(dyg, hidden_all)
    slot_grad = move(total, lambda z, x, y, c: (x, z, y, c))
    grad_tokens = dot(picker, slot_grad, ((0,), (1,))).astype(BF)
    return grad_tokens, grad_gate, grad_up, grad_down


def plane_sum(a, index, order):
    got = [block(a, index)]
    got += [move(block(a, index + j), shift(order, j)) for j in range(1, N)]
    return sum_of(got).astype(BF)


def solution(mesh):
    fine = Mesh(mesh.devices.reshape(N, N, N, 2), ("z", "x", "y", "core"))
    cuts = ("x", "y", "core")
    split, rows = P("z", cuts), P("z", None)
    return jax.shard_map(
        per_device,
        mesh=fine,
        in_specs=(split, split, rows, rows, split, split, split),
        out_specs=(split, split, split, split),
        check_vma=False,
    )
```

```python
import functools

import jax
import jax.numpy as jnp
from jax import lax
from jax.experimental import pallas as pl
from jax.experimental.pallas import tpu as pltpu
from jax.sharding import Mesh
from jax.sharding import PartitionSpec as P

CAP = 384
BF = jnp.bfloat16
F32 = jnp.float32
N = 4


def index_of(z, x, y, c):
    return ((z * N + x) * N + y) * 2 + c


def every(function):
    pairs = []
    for z in range(N):
        for x in range(N):
            for y in range(N):
                for c in range(2):
                    pairs.append((index_of(z, x, y, c), index_of(*function(z, x, y, c))))
    return pairs


def move(a, function):
    return lax.ppermute(a, ("z", "x", "y", "core"), every(function))


def shift(order, j):
    def function(z, x, y, c):
        return (z, x, (y + j) % N, c) if order[c] == "y" else (z, (x + j) % N, y, c)

    return function


def other_core(a):
    return lax.ppermute(a, "core", [(0, 1), (1, 0)])


def along_z(a, k):
    return lax.ppermute(a, "z", [(i, (i + k) % N) for i in range(N)])


def block(a, index):
    return lax.dynamic_index_in_dim(a, index % N, 0, keepdims=False)


def put(a, value, index):
    return lax.dynamic_update_slice(a, value[None], (index % N,) + (0,) * value.ndim)


def cost(flops, nbytes):
    return pl.CostEstimate(flops=int(flops), bytes_accessed=int(nbytes), transcendentals=0)


def params(mib):
    return pltpu.CompilerParams(vmem_limit_bytes=mib * 1024 * 1024)


def dot(a, b, dims):
    return lax.dot_general(a, b, (dims, ((), ())), preferred_element_type=F32)


def places(where):
    core, x, y = where[0], where[1], where[2]
    for operand, side in ((0, core), (1, 1 - core)):
        for j in range(N):
            m = lax.rem(jnp.where(side == 0, y, x) + (N - j), N)
            for b in range(N):
                n = lax.rem(jnp.where(side == 0, x, y) + (N - b), N)
                group = jnp.where(side == 0, n, m)
                row = jnp.where(side == 0, 2 * m, 2 * n + 1)
                yield operand, j, b, group, pl.multiple_of(row * 192, 192)


def forward_kernel(count, where, *refs):
    pieces, weights = refs[:2], refs[2 : 2 + count]
    out, xg = refs[2 + count :]
    for operand, j, b, group, row in places(where):
        xg[group, pl.ds(row, 192), :] = pieces[operand][j, b]
    for p in range(2):
        a = jnp.concatenate([xg[2 * p], xg[2 * p + 1]], axis=1)
        for k in range(count):
            total = dot(weights[k][...], a, ((0,), (0,))).astype(BF)
            for h in range(2):
                out[2 * p + h, k] = total[:, h * CAP : (h + 1) * CAP]


def forward(where, own, sib, *weights):
    count = len(weights)
    vm = pl.BlockSpec(memory_space=pltpu.VMEM)
    return pl.pallas_call(
        functools.partial(forward_kernel, count),
        out_shape=(
            jax.ShapeDtypeStruct((N, count, 512, CAP), BF),
            jax.ShapeDtypeStruct((N, 1536, CAP), BF),
        ),
        in_specs=[pl.BlockSpec(memory_space=pltpu.SMEM)] + [vm] * (2 + count),
        out_specs=(vm, vm),
        compiler_params=params(24),
        cost_estimate=cost(count * 2 * 1536 * 1536 * 512, 5e6 * (1 + count)),
        name="forward_%d" % count,
    )(where, own, sib, *weights)


def slot_kernel(where, wg, wu, dgu, out):
    side = where[0]
    w = jnp.concatenate(
        [
            jnp.concatenate(
                [r[pl.ds(pl.multiple_of((2 * f + side) * 192, 192), 192), :] for f in range(N)]
            )
            for r in (wg, wu)
        ],
        axis=1,
    )
    for p in range(2):
        d = jnp.concatenate(
            [jnp.concatenate([dgu[2 * p + h, k] for k in range(2)]) for h in range(2)], axis=1
        )
        total = dot(w, d, ((1,), (0,))).astype(BF)
        for h in range(2):
            g = 2 * p + h
            for f in range(N):
                index = jnp.where(side == 0, f * N + g, g * N + f)
                out[index] = total[f * 192 : (f + 1) * 192, h * CAP : (h + 1) * CAP]


def slot_partials(side, wg, wu, dgu):
    vm = pl.BlockSpec(memory_space=pltpu.VMEM)
    return pl.pallas_call(
        slot_kernel,
        out_shape=jax.ShapeDtypeStruct((N * N, 192, CAP), BF),
        in_specs=[pl.BlockSpec(memory_space=pltpu.SMEM)] + [vm] * 3,
        out_specs=vm,
        compiler_params=params(24),
        cost_estimate=cost(2 * 1536 * 1536 * 512, 9e6),
        name="slot_partials",
    )(side.reshape(1).astype(jnp.int32), wg, wu, dgu)


def weight_kernel(x, d, *outs):
    for k, out in enumerate(outs):
        total = 0.0
        for p in range(2):
            left = jnp.concatenate([x[2 * p], x[2 * p + 1]], axis=1)
            right = jnp.concatenate([d[2 * p, k], d[2 * p + 1, k]], axis=1)
            total += dot(left, right, ((1,), (1,)))
        out[...] = total.astype(BF)


def weight_grads(x, d):
    n = d.shape[1]
    rows = 256
    return pl.pallas_call(
        weight_kernel,
        grid=(1536 // rows,),
        out_shape=[jax.ShapeDtypeStruct((1536, 512), BF)] * n,
        in_specs=[
            pl.BlockSpec((N, rows, CAP), lambda i: (0, i, 0)),
            pl.BlockSpec((N, n, 512, CAP), lambda i: (0, 0, 0, 0)),
        ],
        out_specs=[pl.BlockSpec((rows, 512), lambda i: (i, 0))] * n,
        compiler_params=params(20),
        cost_estimate=cost(n * 2 * 1536 * 1536 * 512, 8e6),
        name="weight_grads_%d" % n,
    )(x, d)


def start_sum_over_z(a, z):
    far = block(a, z + 2)
    up_half = along_z(far[0], 1)
    down_half = along_z(far[1], 3)
    right, left = block(a, z + 1), block(a, z + 3)
    right = jnp.stack([right[0] + up_half, right[1]])
    left = jnp.stack([left[0], left[1] + down_half])
    return right, left


def finish_sum_over_z(a, right, left, z):
    from_left, from_right = along_z(right, 1), along_z(left, 3)
    return block(a, z).astype(F32) + from_left.astype(F32) + from_right.astype(F32)


def neighbours_over_z(a):
    return along_z(a, 1), along_z(a, 3)


def gather_over_z(a, near, z):
    from_left, from_right = near
    far0 = along_z(from_left[0], 1)
    far1 = along_z(from_right[1], 3)
    out = jnp.zeros((N,) + a.shape, a.dtype)
    out = put(out, a, z)
    out = put(out, from_left, z + 3)
    out = put(out, from_right, z + 1)
    return put(out, jnp.stack([far0, far1]), z + 2)


def sum_of(arrays):
    return sum(a.astype(F32) for a in arrays)


def per_device(tokens, cotangent, expert_ids, gates, w_gate, w_up, w_down):
    z, x, y, core = (lax.axis_index(a) for a in ("z", "x", "y", "core"))
    where = jnp.stack([core, (x - z + N) % N, y]).astype(jnp.int32)
    routed = expert_ids == 0
    routed_weight = jnp.sum(jnp.where(routed, gates, 0.0), axis=1)
    is_routed = jnp.any(routed, axis=1)
    slot_rank = jnp.cumsum(is_routed.astype(jnp.int32)) - 1
    slot_index = jnp.arange(CAP, dtype=jnp.int32)
    selector = (slot_rank[None, :] == slot_index[:, None]) & is_routed[None, :]
    picker = selector.astype(BF)
    slot_weight = jnp.sum(jnp.where(selector, routed_weight[None, :], 0.0), axis=1)
    x_slots = dot(tokens, picker, ((0,), (1,))).astype(BF)
    dy_slots = dot(cotangent, picker, ((0,), (1,))).astype(BF)
    scaled = (slot_weight[None, :] * dy_slots.astype(F32)).astype(BF)

    both = jnp.stack([x_slots, scaled])
    both = move(both, lambda z, x, y, c: (x, (z + x) % N, y, c))
    hop = [both] + [move(both, shift("xy", j)) for j in range(1, N)]
    x_held = jnp.stack([a[0] for a in hop])
    dy_held = jnp.stack([a[1] for a in hop])
    x_own = [x_held] + [move(x_held, shift("yx", j)) for j in range(1, N)]
    dy_held, _ = lax.optimization_barrier((dy_held, x_own[2]))
    x_own = jnp.stack(x_own)
    x_sib = other_core(x_own)
    gu, xg = forward(where, x_own, x_sib, w_gate, w_up)
    dy_own = [dy_held] + [move(dy_held, shift("yx", j)) for j in range(1, N)]
    right, left = start_sum_over_z(gu, z)
    dy_own, _ = lax.optimization_barrier((dy_own, (right, left)))
    dy_own = jnp.stack(dy_own)
    dy_sib = other_core(dy_own)
    gh, dyg = forward(where, dy_own, dy_sib, w_down)
    gate_up = finish_sum_over_z(gu, right, left, z)
    gate_pre, up_pre = gate_up[0], gate_up[1]
    gh = gh.reshape(N, 2, 256, CAP)
    right, left = start_sum_over_z(gh, z)
    grad_hidden = finish_sum_over_z(gh, right, left, z).reshape(512, CAP)

    logistic = jax.nn.sigmoid(gate_pre)
    activated = gate_pre * logistic
    hidden = (activated * up_pre).astype(BF)
    dup = (grad_hidden * activated).astype(BF)
    dgate = (grad_hidden * up_pre * logistic * (1.0 + gate_pre * (1.0 - logistic))).astype(BF)

    dgu = jnp.stack([dgate, dup])
    near = neighbours_over_z(dgu)
    dgu = gather_over_z(dgu, near, z)
    theirs = other_core(slot_partials(1 - core, w_gate, w_up, dgu))
    total = slot_partials(core, w_gate, w_up, dgu)
    total = sum_of((total, theirs)).astype(BF).reshape(N, N, 192, CAP)
    dgu, total = lax.optimization_barrier((dgu, total))
    hidden, _ = lax.optimization_barrier((hidden.reshape(2, 256, CAP), total))
    hidden_near = neighbours_over_z(hidden)
    total = plane_sum(total, jnp.where(core == 0, y, x), "yx")
    hidden_near, _ = lax.optimization_barrier((hidden_near, total))
    hidden_all = gather_over_z(hidden, hidden_near, z).reshape(N, 1, 512, CAP)
    grad_gate, grad_up = weight_grads(xg, dgu)
    total, grad_gate = lax.optimization_barrier((total, grad_gate))
    total = plane_sum(total, jnp.where(core == 0, x, y), "xy")
    (grad_down,) = weight_grads(dyg, hidden_all)
    slot_grad = move(total, lambda z, x, y, c: (x, z, y, c))
    grad_tokens = dot(picker, slot_grad, ((0,), (1,))).astype(BF)
    return grad_tokens, grad_gate, grad_up, grad_down


def plane_sum(a, index, order):
    got = [block(a, index)]
    got += [move(block(a, index + j), shift(order, j)) for j in range(1, N)]
    return sum_of(got).astype(BF)


def solution(mesh):
    fine = Mesh(mesh.devices.reshape(N, N, N, 2), ("z", "x", "y", "core"))
    cuts = ("x", "y", "core")
    split, rows = P("z", cuts), P("z", None)
    return jax.shard_map(
        per_device,
        mesh=fine,
        in_specs=(split, split, rows, rows, split, split, split),
        out_specs=(split, split, split, split),
        check_vma=False,
    )
```
